32 devices in a mesh: row: 4 (over y, x), col: 8 (over z, core).
Axes of the slice: x: 2, y: 2, z: 4, core: 2. Of those that a mesh axis runs over, the one named last changes fastest.
Arguments:
- x_feats: bfloat16 [4096, 128], P(('col', 'row')), may hold values from -6 to 6
- weight: bfloat16 [128, 128], replicated, may hold values from -0.5 to 0.5
- bias: float32 [128], replicated, may hold values from -3 to 3
- block_values: bfloat16 [4, 8, 192, 128, 128], P('row', 'col'), may hold values from -0.0546875 to 0.0546875
- block_rows: int32 [4, 8, 192], P('row', 'col'), may hold values from 0 to 31, as said below
- block_cols: int32 [4, 8, 192], P('row', 'col'), may hold values from 0 to 31, as said below
- block_counts: int32 [4, 8], P('row', 'col'), may hold values from 2 to 192, as said below
- cotangent: bfloat16 [4096, 128], P(('col', 'row')), may hold values from -0.09375 to 0.09375
Outputs:
- activations: bfloat16 [4096, 128], P(('col', 'row'))
- weight_grad: float32 [128, 128], replicated
- bias_grad: float32 [128], replicated
The draws below stay inside these ranges and needn't reach their ends.
Inputs may be any that keep to these rules, and one draw needn't show every extreme that they name: `block_rows`: grid cell (r, c) owns node segment c * 4 + r, the nodes c * 4 * 128 + r * 128 onward. Every slot of cell (r, c), used or not, names a row block inside a segment s with s % 4 == r and a column block inside a segment t with t // 4 == c, and the row block is at most the column block. Pairs may repeat. `block_cols`: see block_rows. `block_counts`: every cell uses at least 2 slots; some cell uses all 192 slots.
All inputs are finite; a program needn't handle non-finite values.
Results may differ from the reference program's by a relative error of at most 0.008.
Values may be sent and summed in bfloat16 or wider, within the bound.
A program may use at most 128 MiB of HBM per device.

```python
import jax
import jax.numpy as jnp
from jax import lax

F_IN = 128
F_OUT = 128
BLOCK = 128
NODE_DEV = 128
BLK_DEV = 192
NODES = 4096
N_ROW = 4
N_COL = 8


def block_plan(key):
    shape = (N_ROW, N_COL, BLK_DEV)
    per_seg = NODE_DEV // 128
    keys = jax.random.split(key, 7)
    rows_here = jnp.broadcast_to(jnp.arange(N_ROW, dtype=jnp.int32)[:, None, None], shape)
    cols_here = jnp.broadcast_to(jnp.arange(N_COL, dtype=jnp.int32)[None, :, None], shape)
    earlier = jax.random.randint(keys[0], shape, 0, cols_here + 1, dtype=jnp.int32)
    same = earlier == cols_here
    later_offset = jax.random.randint(keys[1], shape, 0, N_ROW - rows_here, dtype=jnp.int32) + rows_here
    any_offset = jax.random.randint(keys[2], shape, 0, N_ROW, dtype=jnp.int32)
    offset = jnp.where(same, later_offset, any_offset)
    first = jax.random.randint(keys[3], shape, 0, per_seg, dtype=jnp.int32)
    second_free = jax.random.randint(keys[4], shape, 0, per_seg, dtype=jnp.int32)
    second_tied = first + jax.random.randint(keys[5], shape, 0, per_seg - first, dtype=jnp.int32)
    second = jnp.where(same & (offset == rows_here), second_tied, second_free)
    row_block = (earlier * N_ROW + rows_here) * per_seg + first
    col_block = (cols_here * N_ROW + offset) * per_seg + second
    grid_cols = jnp.broadcast_to(jnp.arange(N_COL, dtype=jnp.int32)[None, :], (N_ROW, N_COL))
    bump = jax.random.randint(keys[6], (N_ROW, N_COL), 0, N_COL, dtype=jnp.int32)
    counts = jnp.minimum(BLK_DEV, jnp.maximum(2, (BLK_DEV * (grid_cols + 1) + bump) // N_COL))
    return (row_block, col_block, counts)


def draw_block_rows(key, part):
    return block_plan(key)[0]


def draw_block_cols(key, part):
    return block_plan(key)[1]


def draw_block_counts(key, part):
    return block_plan(key)[2]


def level_of(own_key, dims, cuts, low, top_value):
    level, own = 1.0, jax.random.fold_in(own_key, 6)
    for position, parts in cuts:
        draws = jnp.exp(jax.random.uniform(jax.random.fold_in(own, position), (parts,), jnp.float32, low / len(cuts), top_value / len(cuts)))
        level = level * jnp.repeat(draws, dims[position] // parts).reshape([-1 if axis == position else 1 for axis in range(len(dims))])
    return level


def normal_values(key, extent, deviation, reach, cuts=(), held_as=jnp.bfloat16):
    result = deviation * jax.random.normal(key, extent, jnp.float32)
    if cuts:
        result = result * level_of(key, extent, cuts, -0.22, 0.18)
    return jnp.clip(result, -reach, reach).astype(held_as)


def setup_inputs(seed: int = 0) -> dict:
    seeds = jax.random.split(jax.random.key(seed), 9)
    return {
        "x_feats": normal_values(seeds[0], (NODES, F_IN), 1.0, 6.0, ((0, 32),)),
        "weight": normal_values(seeds[1], (F_IN, F_OUT), F_IN ** -0.5, 0.5),
        "bias": normal_values(seeds[2], (F_OUT,), 0.5, 3.0, (), jnp.float32),
        "block_values": normal_values(seeds[3], (N_ROW, N_COL, BLK_DEV, BLOCK, BLOCK), (BLK_DEV * 64) ** -0.5, 0.0546875, ((0, 4), (1, 8))),
        "block_rows": draw_block_rows(jax.random.fold_in(seeds[8], 71), 0),
        "block_cols": draw_block_cols(jax.random.fold_in(seeds[8], 71), 0),
        "block_counts": draw_block_counts(jax.random.fold_in(seeds[8], 71), 0),
        "cotangent": normal_values(seeds[7], (NODES, F_OUT), (NODES ** -0.5), 0.09375, ((0, 32),)),
    }


def gelu_parts(pre):
    cdf = 0.5 * (1.0 + lax.erf(pre * 0.7071067811865476))
    dens = jnp.exp(-0.5 * pre * pre) * 0.3989422804014327
    return pre * cdf, cdf + pre * dens


def spread(block_values, block_rows, block_cols, block_counts, feats):
    total_blocks = NODES // BLOCK
    width = feats.shape[1]
    tiles = feats.reshape(total_blocks, BLOCK, width)
    flat_values = block_values.reshape(N_ROW * N_COL, BLK_DEV, BLOCK, BLOCK)
    flat_rows = block_rows.reshape(N_ROW * N_COL, BLK_DEV).astype(jnp.int32)
    flat_cols = block_cols.reshape(N_ROW * N_COL, BLK_DEV).astype(jnp.int32)
    alive = (jnp.arange(BLK_DEV)[None, :] < block_counts.reshape(-1)[:, None]).astype(jnp.float32)

    def advance(accum, item):
        values, rows_id, cols_id, used = item
        matrices = values.astype(jnp.float32) * used[:, None, None]
        forward = jnp.einsum("kab,kbw->kaw", matrices, tiles[cols_id].astype(jnp.float32), precision=lax.Precision.HIGHEST)
        mirror = jnp.einsum("kba,kbw->kaw", matrices, tiles[rows_id].astype(jnp.float32), precision=lax.Precision.HIGHEST)
        accum = accum.at[rows_id].add(forward).at[cols_id].add(mirror)
        return accum, None

    start = jnp.zeros((total_blocks, BLOCK, width), jnp.float32)
    accum, _ = lax.scan(advance, start, (flat_values, flat_rows, flat_cols, alive))
    return accum.reshape(NODES, width)


def reference(x_feats, weight, bias, block_values, block_rows, block_cols, block_counts, cotangent):
    hidden = jnp.dot(x_feats, weight, preferred_element_type=jnp.float32).astype(jnp.bfloat16)
    pre = spread(block_values, block_rows, block_cols, block_counts, hidden) + bias
    act, slope = gelu_parts(pre)
    grad_pre = (cotangent.astype(jnp.float32) * slope).astype(jnp.bfloat16)
    back = spread(block_values, block_rows, block_cols, block_counts, grad_pre)
    weight_grad = jnp.dot(x_feats.astype(jnp.float32).T, back, precision=lax.Precision.HIGHEST)
    bias_grad = jnp.sum(grad_pre.astype(jnp.float32), axis=0)
    return act.astype(jnp.bfloat16), weight_grad, bias_grad
```

```python
import functools

import jax
import jax.numpy as jnp
from jax import lax
from jax.experimental import pallas as pl
from jax.experimental.pallas import tpu as pltpu
from jax.sharding import PartitionSpec as P

F32 = jnp.float32
BF16 = jnp.bfloat16
MESH = pl.DeviceIdType.MESH
MIB = 1024 * 1024


def gelu_parts(pre):
    cdf = 0.5 * (1.0 + lax.erf(pre * 0.7071067811865476))
    dens = jnp.exp(-0.5 * pre * pre) * 0.3989422804014327
    return (pre * cdf, cdf + pre * dens)


def densify(n_row, n_col, chunk, rows_ref, cols_ref, count_ref, values_ref, tiles_ref, held, even, odd, sems):
    block = values_ref.shape[-1]
    tiles = n_row * n_col
    half = n_col // 2
    count = count_ref[0, 0]
    chunks = lax.div(count + chunk - 1, chunk)

    def fetch(i):
        part = pl.ds(i * chunk, chunk)
        return pltpu.make_async_copy(values_ref.at[0, 0, part], held.at[part], sems.at[i])

    @pl.loop(0, chunks)
    def _(i):
        fetch(i).start()

    @pl.loop(0, tiles)
    def _(t):
        even[t] = jnp.zeros((block, block), F32)
        odd[t] = jnp.zeros((block, block), F32)

    @pl.loop(0, chunks)
    def _(i):
        fetch(i).wait()
        for s in range(0, chunk, 2):
            for step, acc in ((0, even), (1, odd)):
                k = i * chunk + s + step
                row = lax.div(rows_ref[0, 0, k], n_row)
                place = lax.rem(row, 2) * half + lax.div(row, 2)
                tile = place * n_row + lax.rem(cols_ref[0, 0, k], n_row)
                tile = jnp.where(k < count, tile, tiles)
                acc[tile] = acc[tile] + held[k].astype(F32)

    for p in range(n_col):
        for q in range(n_row):
            t = p * n_row + q
            tiles_ref[p * block:(p + 1) * block, q * block:(q + 1) * block] = (even[t] + odd[t]).astype(BF16)


def layer(
    n_row, n_col, tiles_ref, x_ref, w_ref, bias_ref, cot_ref, act_ref, wg_ref, bg_ref,
    xcol, xrow, half_out, half_in, sum_out, sum_in, mir_out, mir_in, part, red1, red2, red3,
    s_xrow, r_xrow, s_xz, r_xz, s_xp, r_xp, s_half, r_half, s_sum, r_sum, s_mir, r_mir,
    s_1, r_1, s_2, r_2, s_3, r_3,
):
    r = lax.axis_index("row")
    c = lax.axis_index("col")
    block = x_ref.shape[0]
    n_z = n_col // 2
    z = lax.div(c, 2)
    core = lax.rem(c, 2)
    mate = 1 - core
    mate_id = (r, z * 2 + mate)
    here = core * n_z + z
    n_part, part_rows = part.shape[0], part.shape[1] - 8
    sends = []

    def rows_of(index):
        return pl.ds(pl.multiple_of(index * block, block), block)

    def copy(src, dst, send, recv, device):
        return pltpu.make_async_remote_copy(
            src_ref=src, dst_ref=dst, send_sem=send, recv_sem=recv, device_id=device, device_id_type=MESH
        )

    def send(src, dst, s, t, device):
        one = copy(src, dst, s, t, device)
        one.start()
        sends.append(one)

    def row_at(d):
        return lax.rem(r + d, n_row)

    def z_at(d):
        return lax.rem(z + d, n_z)

    def col_at(d):
        return lax.rem(c + d, n_col)

    barrier = pltpu.get_barrier_semaphore()
    for d in range(1, n_row):
        pl.semaphore_signal(barrier, inc=1, device_id=(row_at(d), c), device_id_type=MESH)
    for d in range(1, n_col):
        pl.semaphore_signal(barrier, inc=1, device_id=(r, col_at(d)), device_id_type=MESH)
    x = x_ref[...]
    xcol[rows_of(r), :] = x
    xrow[here] = x.T
    pl.semaphore_wait(barrier, n_row + n_col - 2)

    for d in range(1, n_row):
        send(xcol.at[rows_of(r)], xcol.at[rows_of(r)], s_xrow.at[d - 1], r_xrow.at[d - 1], (row_at(d), c))
    for d in range(1, n_z):
        send(xrow.at[here], xrow.at[here], s_xz.at[d - 1], r_xz.at[d - 1], (r, z_at(d) * 2 + core))
    send(xrow.at[here], xrow.at[here], s_xp.at[0], r_xp.at[0], mate_id)

    for d in range(1, n_row):
        slot = xcol.at[rows_of(row_at(n_row - d))]
        copy(slot, slot, s_xrow.at[d - 1], r_xrow.at[d - 1], (row_at(d), c)).wait_recv()

    span = n_z * block
    there = tiles_ref[pl.ds(pl.multiple_of(mate * span, span), span), :]
    xc = xcol[...]
    half_out[...] = jnp.dot(there, xc, preferred_element_type=F32).astype(BF16)
    send(half_out, half_in, s_half.at[0], r_half.at[0], mate_id)
    mine = tiles_ref[pl.ds(pl.multiple_of(core * span, span), span), :]
    own = jnp.dot(mine, xc, preferred_element_type=F32)

    for d in range(1, n_z):
        slot = xrow.at[core * n_z + z_at(n_z - d)]
        copy(slot, slot, s_xz.at[d - 1], r_xz.at[d - 1], mate_id).wait_recv()
        send(slot, slot, s_xp.at[d], r_xp.at[d], mate_id)

    copy(half_out, half_in, s_half.at[0], r_half.at[0], mate_id).wait_recv()
    total = (own + half_in[...].astype(F32)).astype(BF16)
    sum_out[...] = total
    for d in range(1, n_z):
        send(
            sum_out.at[rows_of(z_at(d))], sum_in.at[d - 1], s_sum.at[d - 1], r_sum.at[d - 1],
            (r, z_at(d) * 2 + core),
        )

    for d in range(n_z):
        slot = xrow.at[mate * n_z + z_at(n_z - d)]
        copy(slot, slot, s_xp.at[d], r_xp.at[d], mate_id).wait_recv()

    xt = jnp.concatenate([xrow[i] for i in range(n_col)], axis=1)
    for q in range(n_row // 2):
        both = jnp.dot(xt, tiles_ref[:, 2 * q * block:2 * (q + 1) * block], preferred_element_type=F32).astype(BF16)
        mir_out[2 * q] = both[:, :block]
        mir_out[2 * q + 1] = both[:, block:]
    for d in range(1, n_row):
        send(mir_out.at[row_at(d)], mir_in.at[d - 1], s_mir.at[d - 1], r_mir.at[d - 1], (row_at(d), c))

    y = sum_out[rows_of(z), :].astype(F32)
    for d in range(1, n_z):
        copy(sum_in.at[d - 1], sum_in.at[d - 1], s_sum.at[d - 1], r_sum.at[d - 1], mate_id).wait_recv()
        y = y + sum_in[d - 1].astype(F32)
    yt = mir_out[r].astype(F32)
    for d in range(1, n_row):
        copy(mir_in.at[d - 1], mir_in.at[d - 1], s_mir.at[d - 1], r_mir.at[d - 1], mate_id).wait_recv()
        yt = yt + mir_in[d - 1].astype(F32)
    y = y + yt.T

    high = y.astype(BF16)
    low = (y - high.astype(F32)).astype(BF16)
    w = w_ref[...]
    pre = (
        jnp.dot(high, w, preferred_element_type=F32)
        + jnp.dot(low, w, preferred_element_type=F32)
        + bias_ref[...].reshape(1, -1)
    )
    act, slope = gelu_parts(pre)
    act_ref[...] = act.astype(BF16)
    grad = (cot_ref[...].astype(F32) * slope).astype(BF16)
    local = jnp.dot(high.T, grad, preferred_element_type=F32) + jnp.dot(low.T, grad, preferred_element_type=F32)
    local_bias = jnp.broadcast_to(jnp.sum(grad.astype(F32), axis=0, keepdims=True), (8, grad.shape[1]))
    for j in range(n_part):
        part[j, :part_rows, :] = local[j * part_rows:(j + 1) * part_rows, :]
        part[j, part_rows:, :] = local_bias

    red1[c] = part[lax.rem(c, n_part)]
    for d in range(1, n_col):
        to = col_at(d)
        send(part.at[lax.rem(to, n_part)], red1.at[c], s_1.at[d - 1], r_1.at[d - 1], (r, to))
    for d in range(1, n_col):
        slot = red1.at[col_at(n_col - d)]
        copy(slot, slot, s_1.at[d - 1], r_1.at[d - 1], mate_id).wait_recv()
    red2[r] = functools.reduce(lambda a, b: a + b, [red1[i] for i in range(n_col)])
    for d in range(1, n_row):
        send(red2.at[r], red2.at[r], s_2.at[d - 1], r_2.at[d - 1], (row_at(d), c))
    for d in range(1, n_row):
        slot = red2.at[row_at(n_row - d)]
        copy(slot, slot, s_2.at[d - 1], r_2.at[d - 1], mate_id).wait_recv()
    done = functools.reduce(lambda a, b: a + b, [red2[i] for i in range(n_row)])
    bg_ref[...] = done[part_rows:part_rows + 1, :]
    red3[c] = done[:part_rows, :]
    for d in range(1, n_col):
        send(red3.at[c], red3.at[c], s_3.at[d - 1], r_3.at[d - 1], (r, col_at(d)))
    for d in range(1, n_col):
        slot = red3.at[col_at(n_col - d)]
        copy(slot, slot, s_3.at[d - 1], r_3.at[d - 1], mate_id).wait_recv()
    for j in range(n_part):
        wg_ref[j * part_rows:(j + 1) * part_rows, :] = red3[j]
    for one in sends:
        one.wait_send()


def on_device(n_row, n_col, x_feats, weight, bias, block_values, block_rows, block_cols, block_counts, cotangent):
    slots, block = block_values.shape[2], block_values.shape[-1]
    nodes, f_in = x_feats.shape
    f_out = weight.shape[1]
    assert nodes == block and n_col % 2 == 0 and n_row % 2 == 0
    tiles = n_row * n_col
    chunk = 16 if slots % 16 == 0 else slots
    vmem = pl.BlockSpec(memory_space=pltpu.VMEM)
    smem = pl.BlockSpec(memory_space=pltpu.SMEM)
    dense_bytes = slots * block * block * 2 + (2 * (tiles + 1) * 4 + tiles * 2) * block * block
    dense = pl.pallas_call(
        functools.partial(densify, n_row, n_col, chunk),
        out_shape=jax.ShapeDtypeStruct((n_col * block, n_row * block), BF16),
        in_specs=[smem, smem, smem, pl.BlockSpec(memory_space=pl.ANY)],
        out_specs=vmem,
        scratch_shapes=[
            pltpu.VMEM((slots, block, block), BF16),
            pltpu.VMEM((tiles + 1, block, block), F32),
            pltpu.VMEM((tiles + 1, block, block), F32),
            pltpu.SemaphoreType.DMA((slots // chunk,)),
        ],
        compiler_params=pltpu.CompilerParams(vmem_limit_bytes=dense_bytes + 4 * MIB),
        cost_estimate=pl.CostEstimate(flops=slots * block * block, bytes_accessed=slots * block * block * 2, transcendentals=0),
        name="densify",
    )(block_rows, block_cols, block_counts, block_values)

    n_z = n_col // 2
    n_part = min(n_col, f_in // 8)
    part_rows = f_in // n_part
    pairs = []
    for count in (n_row - 1, n_z - 1, n_z, 1, n_z - 1, n_row - 1, n_col - 1, n_row - 1, n_col - 1):
        pairs += [pltpu.SemaphoreType.DMA((count,))] * 2
    act, weight_grad, bias_grad = pl.pallas_call(
        functools.partial(layer, n_row, n_col),
        out_shape=(
            jax.ShapeDtypeStruct((nodes, f_out), BF16),
            jax.ShapeDtypeStruct((f_in, f_out), F32),
            jax.ShapeDtypeStruct((1, f_out), F32),
        ),
        in_specs=[vmem] * 5,
        out_specs=(vmem, vmem, vmem),
        scratch_shapes=[
            pltpu.VMEM((n_row * block, f_in), BF16),
            pltpu.VMEM((n_col, f_in, block), BF16),
            pltpu.VMEM((n_z * block, f_in), BF16),
            pltpu.VMEM((n_z * block, f_in), BF16),
            pltpu.VMEM((n_z * block, f_in), BF16),
            pltpu.VMEM((n_z - 1, block, f_in), BF16),
            pltpu.VMEM((n_row, f_in, block), BF16),
            pltpu.VMEM((n_row - 1, f_in, block), BF16),
            pltpu.VMEM((n_part, part_rows + 8, f_out), F32),
            pltpu.VMEM((n_col, part_rows + 8, f_out), F32),
            pltpu.VMEM((n_row, part_rows + 8, f_out), F32),
            pltpu.VMEM((n_col, part_rows, f_out), F32),
            *pairs,
        ],
        compiler_params=pltpu.CompilerParams(
            collective_id=0, has_side_effects=True, vmem_limit_bytes=tiles * block * block * 2 + 16 * MIB
        ),
        cost_estimate=pl.CostEstimate(
            flops=4 * tiles * block * block * f_in, bytes_accessed=tiles * block * block * 2, transcendentals=0
        ),
        name="layer",
    )(dense, x_feats, weight, bias, cotangent)
    return act, weight_grad, bias_grad.reshape(f_out)


def solution(mesh):
    in_specs = (
        P(("col", "row"), None),
        P(),
        P(),
        P("row", "col", None, None, None),
        P("row", "col", None),
        P("row", "col", None),
        P("row", "col"),
        P(("col", "row"), None),
    )
    out_specs = (P(("col", "row"), None), P(), P())
    return jax.shard_map(
        functools.partial(on_device, mesh.shape["row"], mesh.shape["col"]),
        mesh=mesh, in_specs=in_specs, out_specs=out_specs, check_vma=False,
    )
```

```python
import functools

import jax
import jax.numpy as jnp
from jax import lax
from jax.experimental import pallas as pl
from jax.experimental.pallas import tpu as pltpu
from jax.sharding import PartitionSpec as P

F32 = jnp.float32
BF16 = jnp.bfloat16
MESH = pl.DeviceIdType.MESH
MIB = 1024 * 1024


def gelu_parts(pre):
    cdf = 0.5 * (1.0 + lax.erf(pre * 0.7071067811865476))
    dens = jnp.exp(-0.5 * pre * pre) * 0.3989422804014327
    return (pre * cdf, cdf + pre * dens)


def sort_slots(n_row, n_col, rows_ref, cols_ref, count_ref, keys, order):
    slots = rows_ref.shape[-1]
    log_row = n_row.bit_length() - 1
    row = jnp.right_shift(rows_ref[0], log_row)
    place = jnp.bitwise_and(row, 1) * (n_col // 2) + jnp.right_shift(row, 1)
    tile = place * n_row + jnp.bitwise_and(cols_ref[0], n_row - 1)
    index = lax.broadcasted_iota(jnp.int32, (1, slots), 1)
    tile = jnp.where(index < count_ref[...], tile, n_row * n_col)
    keys[...] = n_row * n_col * 256 + lax.broadcasted_iota(jnp.int32, keys.shape, 1)
    keys[0:1, 0:slots] = tile * 256 + index
    along = jnp.broadcast_to(keys[0:1, :], (256, 256))
    down = along.T
    rank = jnp.sum((along < down).astype(jnp.int32), axis=1, keepdims=True)
    lane = lax.broadcasted_iota(jnp.int32, (256, 256), 1)
    order[0:1, :] = jnp.sum(jnp.where(rank == lane, down, 0), axis=0, keepdims=True)
    order[1:2, :] = jnp.sum((jnp.right_shift(down, 8) <= lane).astype(jnp.int32), axis=0, keepdims=True)
    order[2:, :] = jnp.zeros((order.shape[0] - 2, 256), jnp.int32)


def build_tiles(n_row, n_col, order, held, runs, tiles_ref):
    slots, block = held.shape[0], held.shape[1]

    def step(i, carry):
        total, before = carry
        key = order[0, i]
        tile = jnp.right_shift(key, 8)
        slot = jnp.minimum(jnp.bitwise_and(key, 255), slots - 1)
        total = jnp.where(tile == before, total, 0.0) + held[slot].astype(F32)
        runs[i] = total.astype(BF16)
        return total, tile

    lax.fori_loop(0, slots, step, (jnp.zeros((block, block), F32), jnp.int32(-1)), unroll=4)

    def place(p, before):
        for q in range(n_row):
            end = order[1, p * n_row + q]
            value = runs[jnp.maximum(end - 1, 0)]
            rows = pl.ds(pl.multiple_of(p * block, block), block)
            tiles_ref[rows, q * block:(q + 1) * block] = jnp.where(end > before, value, jnp.zeros_like(value))
            before = end
        return before

    lax.fori_loop(0, n_col, place, jnp.int32(0))


def layer(
    n_row, n_col, rows_ref, cols_ref, count_ref, values_ref, x_ref, w_ref, bias_ref, cot_ref,
    act_ref, wg_ref, bg_ref,
    held, runs, tiles_ref, keys, order, order_smem, values_sem, order_sem,
    xcol, xrow, half_out, half_in, sum_out, sum_in, mir_out, mir_in, pair_out, pair_in, over_z, over_row, final,
    s_xrow, r_xrow, s_xz, r_xz, s_xp, r_xp, s_half, r_half, s_sum, r_sum, s_mir, r_mir,
    s_1, r_1, s_2, r_2, s_3, r_3, s_4, r_4,
):
    fetch = pltpu.make_async_copy(values_ref.at[0, 0], held, values_sem)
    fetch.start()
    r = lax.axis_index("row")
    c = lax.axis_index("col")
    block = x_ref.shape[0]
    n_z = n_col // 2
    z = lax.div(c, 2)
    core = lax.rem(c, 2)
    mate = 1 - core
    mate_id = (r, z * 2 + mate)
    here = core * n_z + z
    sends = []

    def rows_of(index):
        return pl.ds(pl.multiple_of(index * block, block), block)

    def copy(src, dst, send, recv, device):
        return pltpu.make_async_remote_copy(
            src_ref=src, dst_ref=dst, send_sem=send, recv_sem=recv, device_id=device, device_id_type=MESH
        )

    def send(src, dst, s, t, device):
        one = copy(src, dst, s, t, device)
        one.start()
        sends.append(one)

    def row_at(d):
        return lax.rem(r + d, n_row)

    def z_at(d):
        return lax.rem(z + d, n_z)

    barrier = pltpu.get_barrier_semaphore()
    for d in range(1, n_row):
        pl.semaphore_signal(barrier, inc=1, device_id=(row_at(d), c), device_id_type=MESH)
    for d in range(1, n_z):
        pl.semaphore_signal(barrier, inc=1, device_id=(r, z_at(d) * 2 + core), device_id_type=MESH)
    pl.semaphore_signal(barrier, inc=1, device_id=mate_id, device_id_type=MESH)
    x = x_ref[...]
    xcol[rows_of(r), :] = x
    xrow[here] = x.T
    sort_slots(n_row, n_col, rows_ref, cols_ref, count_ref, keys, order)
    to_smem = pltpu.make_async_copy(order, order_smem, order_sem)
    to_smem.start()
    pl.semaphore_wait(barrier, n_row + n_z - 1)

    for d in range(1, n_row):
        send(xcol.at[rows_of(r)], xcol.at[rows_of(r)], s_xrow.at[d - 1], r_xrow.at[d - 1], (row_at(d), c))
    for d in range(1, n_z):
        send(xrow.at[here], xrow.at[here], s_xz.at[d - 1], r_xz.at[d - 1], (r, z_at(d) * 2 + core))
    send(xrow.at[here], xrow.at[here], s_xp.at[0], r_xp.at[0], mate_id)

    to_smem.wait()
    fetch.wait()
    build_tiles(n_row, n_col, order_smem, held, runs, tiles_ref)

    for d in range(1, n_row):
        slot = xcol.at[rows_of(row_at(n_row - d))]
        copy(slot, slot, s_xrow.at[d - 1], r_xrow.at[d - 1], (row_at(d), c)).wait_recv()

    span = n_z * block
    there = tiles_ref[pl.ds(pl.multiple_of(mate * span, span), span), :]
    xc = xcol[...]
    half_out[...] = jnp.dot(there, xc, preferred_element_type=F32).astype(BF16)
    send(half_out, half_in, s_half.at[0], r_half.at[0], mate_id)
    mine = tiles_ref[pl.ds(pl.multiple_of(core * span, span), span), :]
    own = jnp.dot(mine, xc, preferred_element_type=F32)

    for d in range(1, n_z):
        slot = xrow.at[core * n_z + z_at(n_z - d)]
        copy(slot, slot, s_xz.at[d - 1], r_xz.at[d - 1], mate_id).wait_recv()
        send(slot, slot, s_xp.at[d], r_xp.at[d], mate_id)

    copy(half_out, half_in, s_half.at[0], r_half.at[0], mate_id).wait_recv()
    total = (own + half_in[...].astype(F32)).astype(BF16)
    sum_out[...] = total
    for d in range(1, n_z):
        send(
            sum_out.at[rows_of(z_at(d))], sum_in.at[d - 1], s_sum.at[d - 1], r_sum.at[d - 1],
            (r, z_at(d) * 2 + core),
        )

    for d in range(n_z):
        slot = xrow.at[mate * n_z + z_at(n_z - d)]
        copy(slot, slot, s_xp.at[d], r_xp.at[d], mate_id).wait_recv()

    xt = jnp.concatenate([xrow[i] for i in range(n_col)], axis=1)
    for q in range(n_row // 2):
        both = jnp.dot(xt, tiles_ref[:, 2 * q * block:2 * (q + 1) * block], preferred_element_type=F32).astype(BF16)
        mir_out[2 * q] = both[:, :block]
        mir_out[2 * q + 1] = both[:, block:]
    for d in range(1, n_row):
        send(mir_out.at[row_at(d)], mir_in.at[d - 1], s_mir.at[d - 1], r_mir.at[d - 1], (row_at(d), c))

    y = sum_out[rows_of(z), :].astype(F32)
    for d in range(1, n_z):
        copy(sum_in.at[d - 1], sum_in.at[d - 1], s_sum.at[d - 1], r_sum.at[d - 1], mate_id).wait_recv()
        y = y + sum_in[d - 1].astype(F32)
    yt = mir_out[r].astype(F32)
    for d in range(1, n_row):
        copy(mir_in.at[d - 1], mir_in.at[d - 1], s_mir.at[d - 1], r_mir.at[d - 1], mate_id).wait_recv()
        yt = yt + mir_in[d - 1].astype(F32)
    y = y + yt.T

    high = y.astype(BF16)
    low = (y - high.astype(F32)).astype(BF16)
    w = w_ref[...]
    pre = (
        jnp.dot(high, w, preferred_element_type=F32)
        + jnp.dot(low, w, preferred_element_type=F32)
        + bias_ref[...].reshape(1, -1)
    )
    act, slope = gelu_parts(pre)
    act_ref[...] = act.astype(BF16)
    grad = (cot_ref[...].astype(F32) * slope).astype(BF16)
    local = jnp.dot(high.T, grad, preferred_element_type=F32) + jnp.dot(low.T, grad, preferred_element_type=F32)
    bias_sum = jnp.sum(grad.astype(F32), axis=0, keepdims=True)

    f_out = grad.shape[1]
    h = local.shape[0] // 2
    line = lax.broadcasted_iota(jnp.int32, (16, f_out), 0)

    def packed(weight_terms, bias_terms):
        upper = bias_terms.astype(BF16).astype(F32)
        tail = jnp.where(line == 0, upper, jnp.where(line == 1, bias_terms - upper, 0.0))
        return jnp.concatenate([weight_terms, tail], axis=0).astype(BF16)

    def summed(ref):
        total = functools.reduce(lambda a, b: a + b, [ref[i].astype(F32) for i in range(ref.shape[0])])
        return total[:h, :], total[h:h + 1, :] + total[h + 1:h + 2, :]

    for j in range(2):
        pair_out[j, :h, :] = local[j * h:(j + 1) * h, :]
        pair_out[j, h:, :] = jnp.broadcast_to(bias_sum, (8, f_out))
    send(pair_out.at[mate], pair_in, s_1.at[0], r_1.at[0], mate_id)
    copy(pair_in, pair_in, s_1.at[0], r_1.at[0], mate_id).wait_recv()
    both = pair_out[core] + pair_in[...]
    over_z[z] = packed(both[:h, :], both[h:h + 1, :])
    for d in range(1, n_z):
        send(over_z.at[z], over_z.at[z], s_2.at[d - 1], r_2.at[d - 1], (r, z_at(d) * 2 + core))
    for d in range(1, n_z):
        slot = over_z.at[z_at(n_z - d)]
        copy(slot, slot, s_2.at[d - 1], r_2.at[d - 1], mate_id).wait_recv()
    over_row[r] = packed(*summed(over_z))
    for d in range(1, n_row):
        send(over_row.at[r], over_row.at[r], s_3.at[d - 1], r_3.at[d - 1], (row_at(d), c))
    for d in range(1, n_row):
        slot = over_row.at[row_at(n_row - d)]
        copy(slot, slot, s_3.at[d - 1], r_3.at[d - 1], mate_id).wait_recv()
    weight_sum, bias_total = summed(over_row)
    bg_ref[...] = bias_total
    final[core] = weight_sum
    send(final.at[core], final.at[core], s_4.at[0], r_4.at[0], mate_id)
    slot = final.at[mate]
    copy(slot, slot, s_4.at[0], r_4.at[0], mate_id).wait_recv()
    for j in range(2):
        wg_ref[j * h:(j + 1) * h, :] = final[j]
    for one in sends:
        one.wait_send()


def finish(act_ref, wg_ref, bg_ref, act_out, wg_out, bg_out, sems):
    copies = [
        pltpu.make_async_copy(src, dst, sems.at[i])
        for i, (src, dst) in enumerate(((act_ref, act_out), (wg_ref, wg_out), (bg_ref, bg_out)))
    ]
    for one in copies:
        one.start()
    for one in copies:
        one.wait()


def on_device(n_row, n_col, x_feats, weight, bias, block_values, block_rows, block_cols, block_counts, cotangent):
    slots, block = block_values.shape[2], block_values.shape[-1]
    nodes, f_in = x_feats.shape
    f_out = weight.shape[1]
    assert nodes == block and slots <= 256 and n_row * n_col <= 256
    assert n_col % 2 == 0 and n_row % 2 == 0 and n_row & (n_row - 1) == 0
    tiles = n_row * n_col
    vmem = pl.BlockSpec(memory_space=pltpu.VMEM)
    n_z = n_col // 2
    half = f_in // 2
    pairs = []
    for count in (n_row - 1, n_z - 1, n_z, 1, n_z - 1, n_row - 1, 1, n_z - 1, n_row - 1, 1):
        pairs += [pltpu.SemaphoreType.DMA((count,))] * 2
    act, weight_grad, bias_grad = pl.pallas_call(
        functools.partial(layer, n_row, n_col),
        out_shape=(
            jax.ShapeDtypeStruct((nodes, f_out), BF16),
            jax.ShapeDtypeStruct((f_in, f_out), F32),
            jax.ShapeDtypeStruct((1, f_out), F32),
        ),
        in_specs=[vmem] * 3 + [pl.BlockSpec(memory_space=pl.ANY)] + [vmem] * 4,
        out_specs=(vmem, vmem, vmem),
        scratch_shapes=[
            pltpu.VMEM((slots, block, block), BF16),
            pltpu.VMEM((slots, block, block), BF16),
            pltpu.VMEM((n_col * block, n_row * block), BF16),
            pltpu.VMEM((8, 256), jnp.int32),
            pltpu.VMEM((8, 256), jnp.int32),
            pltpu.SMEM((8, 256), jnp.int32),
            pltpu.SemaphoreType.DMA,
            pltpu.SemaphoreType.DMA,
            pltpu.VMEM((n_row * block, f_in), BF16),
            pltpu.VMEM((n_col, f_in, block), BF16),
            pltpu.VMEM((n_z * block, f_in), BF16),
            pltpu.VMEM((n_z * block, f_in), BF16),
            pltpu.VMEM((n_z * block, f_in), BF16),
            pltpu.VMEM((n_z - 1, block, f_in), BF16),
            pltpu.VMEM((n_row, f_in, block), BF16),
            pltpu.VMEM((n_row - 1, f_in, block), BF16),
            pltpu.VMEM((2, half + 8, f_out), F32),
            pltpu.VMEM((half + 8, f_out), F32),
            pltpu.VMEM((n_z, half + 16, f_out), BF16),
            pltpu.VMEM((n_row, half + 16, f_out), BF16),
            pltpu.VMEM((2, half, f_out), F32),
            *pairs,
        ],
        compiler_params=pltpu.CompilerParams(
            collective_id=0, has_side_effects=True, vmem_limit_bytes=58 * MIB
        ),
        cost_estimate=pl.CostEstimate(
            flops=4 * tiles * block * block * f_in, bytes_accessed=tiles * block * block * 2, transcendentals=0
        ),
        name="layer",
    )(block_rows, block_cols, block_counts, block_values, x_feats, weight, bias, cotangent)
    act, weight_grad, bias_grad = pl.pallas_call(
        finish,
        out_shape=tuple(jax.ShapeDtypeStruct(a.shape, a.dtype) for a in (act, weight_grad, bias_grad)),
        in_specs=[vmem] * 3,
        out_specs=(pl.BlockSpec(memory_space=pl.ANY),) * 3,
        scratch_shapes=[pltpu.SemaphoreType.DMA((3,))],
        name="finish",
    )(act, weight_grad, bias_grad)
    return act, weight_grad, bias_grad.reshape(f_out)


def solution(mesh):
    in_specs = (
        P(("col", "row"), None),
        P(),
        P(),
        P("row", "col", None, None, None),
        P("row", "col", None),
        P("row", "col", None),
        P("row", "col"),
        P(("col", "row"), None),
    )
    out_specs = (P(("col", "row"), None), P(), P())
    return jax.shard_map(
        functools.partial(on_device, mesh.shape["row"], mesh.shape["col"]),
        mesh=mesh, in_specs=in_specs, out_specs=out_specs, check_vma=False,
    )
```

```python
import functools

import jax
import jax.numpy as jnp
from jax import lax
from jax.experimental import pallas as pl
from jax.experimental.pallas import tpu as pltpu
from jax.sharding import PartitionSpec as P

F32 = jnp.float32
BF16 = jnp.bfloat16
MESH = pl.DeviceIdType.MESH
MIB = 1024 * 1024


def gelu_parts(pre):
    cdf = 0.5 * (1.0 + lax.erf(pre * 0.7071067811865476))
    dens = jnp.exp(-0.5 * pre * pre) * 0.3989422804014327
    return (pre * cdf, cdf + pre * dens)


def sort_slots(n_row, n_col, rows_ref, cols_ref, count_ref, keys, order):
    slots = rows_ref.shape[-1]
    log_row = n_row.bit_length() - 1
    row = jnp.right_shift(rows_ref[...], log_row)
    place = jnp.bitwise_and(row, 1) * (n_col // 2) + jnp.right_shift(row, 1)
    tile = place * n_row + jnp.bitwise_and(cols_ref[...], n_row - 1)
    index = lax.broadcasted_iota(jnp.int32, (1, slots), 1)
    tile = jnp.where(index < count_ref[...], tile, n_row * n_col)
    keys[...] = n_row * n_col * 256 + lax.broadcasted_iota(jnp.int32, keys.shape, 1)
    keys[0:1, 0:slots] = tile * 256 + index
    along = jnp.broadcast_to(keys[0:1, :], (256, 256))
    down = along.T
    rank = jnp.sum((along < down).astype(jnp.int32), axis=1, keepdims=True)
    lane = lax.broadcasted_iota(jnp.int32, (256, 256), 1)
    order[0:1, :] = jnp.sum(jnp.where(rank == lane, down, 0), axis=0, keepdims=True)
    order[1:2, :] = jnp.sum((jnp.right_shift(down, 8) <= lane).astype(jnp.int32), axis=0, keepdims=True)
    order[2:, :] = jnp.zeros((order.shape[0] - 2, 256), jnp.int32)


def build_tiles(n_row, n_col, order, held, runs, tiles_ref):
    slots, block = held.shape[0], held.shape[1]

    def step(i, carry):
        total, before = carry
        key = order[0, i]
        tile = jnp.right_shift(key, 8)
        slot = jnp.minimum(jnp.bitwise_and(key, 255), slots - 1)
        total = jnp.where(tile == before, total, 0.0) + held[slot].astype(F32)
        runs[i] = total.astype(BF16)
        return total, tile

    lax.fori_loop(0, slots, step, (jnp.zeros((block, block), F32), jnp.int32(-1)), unroll=4)

    def place(p, before):
        for q in range(n_row):
            end = order[1, p * n_row + q]
            value = runs[jnp.maximum(end - 1, 0)]
            rows = pl.ds(pl.multiple_of(p * block, block), block)
            tiles_ref[rows, q * block:(q + 1) * block] = jnp.where(end > before, value, jnp.zeros_like(value))
            before = end
        return before

    lax.fori_loop(0, n_col, place, jnp.int32(0))


def layer(
    n_row, n_col, rows_hbm, cols_hbm, count_hbm, values_hbm, x_hbm, w_hbm, bias_hbm, cot_hbm,
    act_ref, wg_ref, bg_ref,
    rows_ref, cols_ref, count_ref, x_ref, w_ref, bias_ref, cot_ref, input_sems,
    held, runs, tiles_ref, keys, order, order_smem, values_sem, order_sem,
    xcol, xrow, half_out, half_in, sum_out, sum_in, mir_out, mir_in, pair_out, pair_in, over_z, over_row, final,
    s_xrow, r_xrow, s_xz, r_xz, s_xp, r_xp, s_half, r_half, s_sum, r_sum, s_mir, r_mir,
    s_1, r_1, s_2, r_2, s_3, r_3, s_4, r_4,
):
    r = lax.axis_index("row")
    c = lax.axis_index("col")
    block = x_ref.shape[0]
    n_z = n_col // 2
    z = lax.div(c, 2)
    core = lax.rem(c, 2)
    mate = 1 - core
    mate_id = (r, z * 2 + mate)
    here = core * n_z + z
    sends = []

    def rows_of(index):
        return pl.ds(pl.multiple_of(index * block, block), block)

    def copy(src, dst, send, recv, device):
        return pltpu.make_async_remote_copy(
            src_ref=src, dst_ref=dst, send_sem=send, recv_sem=recv, device_id=device, device_id_type=MESH
        )

    def send(src, dst, s, t, device):
        one = copy(src, dst, s, t, device)
        one.start()
        sends.append(one)

    def row_order(t):
        self_at = lax.rem(2 * r + 1, n_row)
        t = jnp.where(t < self_at, t, t + 1)
        return lax.rem(2 * n_row - 1 - r + t, n_row)

    def z_order(t):
        up = jnp.where(n_z - 1 - t > z, n_z - 1 - t, n_z - 2 - t)
        down = jnp.where(t < z, t, t + 1)
        return jnp.where(z < n_z // 2, up, down)

    def row_offset(p):
        return lax.rem(p - r + n_row, n_row) - 1

    def z_offset(p):
        return lax.rem(p - z + n_z, n_z) - 1

    def row_at(d):
        return lax.rem(r + d, n_row)

    def z_at(d):
        return lax.rem(z + d, n_z)

    barrier = pltpu.get_barrier_semaphore()
    for d in range(1, n_row):
        pl.semaphore_signal(barrier, inc=1, device_id=(row_at(d), c), device_id_type=MESH)
    for d in range(1, n_z):
        pl.semaphore_signal(barrier, inc=1, device_id=(r, z_at(d) * 2 + core), device_id_type=MESH)
    pl.semaphore_signal(barrier, inc=1, device_id=mate_id, device_id_type=MESH)
    inputs = [
        pltpu.make_async_copy(src, dst, input_sems.at[i])
        for i, (src, dst) in enumerate((
            (x_hbm, x_ref), (rows_hbm.at[0], rows_ref), (cols_hbm.at[0], cols_ref), (count_hbm, count_ref),
            (w_hbm, w_ref), (bias_hbm, bias_ref), (cot_hbm, cot_ref),
        ))
    ]
    for one in inputs:
        one.start()
    fetch = pltpu.make_async_copy(values_hbm.at[0, 0], held, values_sem)
    fetch.start()
    for one in inputs:
        one.wait()
    x = x_ref[...]
    xcol[rows_of(r), :] = x
    xrow[here] = x.T
    sort_slots(n_row, n_col, rows_ref, cols_ref, count_ref, keys, order)
    to_smem = pltpu.make_async_copy(order, order_smem, order_sem)
    to_smem.start()
    pl.semaphore_wait(barrier, n_row + n_z - 1)

    for t in range(n_z - 1):
        p = z_order(t)
        send(xrow.at[here], xrow.at[here], s_xz.at[z_offset(p)], r_xz.at[z_offset(p)], (r, p * 2 + core))
    for t in range(n_row - 1):
        p = row_order(t)
        d = row_offset(p)
        send(xcol.at[rows_of(r)], xcol.at[rows_of(r)], s_xrow.at[d], r_xrow.at[d], (p, c))
    send(xrow.at[here], xrow.at[here], s_xp.at[0], r_xp.at[0], mate_id)

    to_smem.wait()
    fetch.wait()
    build_tiles(n_row, n_col, order_smem, held, runs, tiles_ref)

    for d in range(1, n_row):
        slot = xcol.at[rows_of(row_at(n_row - d))]
        copy(slot, slot, s_xrow.at[d - 1], r_xrow.at[d - 1], (row_at(d), c)).wait_recv()

    span = n_z * block
    there = tiles_ref[pl.ds(pl.multiple_of(mate * span, span), span), :]
    xc = xcol[...]
    half_out[...] = jnp.dot(there, xc, preferred_element_type=F32).astype(BF16)
    send(half_out, half_in, s_half.at[0], r_half.at[0], mate_id)
    mine = tiles_ref[pl.ds(pl.multiple_of(core * span, span), span), :]
    own = jnp.dot(mine, xc, preferred_element_type=F32)

    for d in range(1, n_z):
        slot = xrow.at[core * n_z + z_at(n_z - d)]
        copy(slot, slot, s_xz.at[d - 1], r_xz.at[d - 1], mate_id).wait_recv()
        send(slot, slot, s_xp.at[d], r_xp.at[d], mate_id)

    copy(half_out, half_in, s_half.at[0], r_half.at[0], mate_id).wait_recv()
    total = (own + half_in[...].astype(F32)).astype(BF16)
    sum_out[...] = total
    for t in range(n_z - 1):
        p = z_order(t)
        d = z_offset(p)
        send(sum_out.at[rows_of(p)], sum_in.at[d], s_sum.at[d], r_sum.at[d], (r, p * 2 + core))

    for d in range(n_z):
        slot = xrow.at[mate * n_z + z_at(n_z - d)]
        copy(slot, slot, s_xp.at[d], r_xp.at[d], mate_id).wait_recv()

    xt = jnp.concatenate([xrow[i] for i in range(n_col)], axis=1)
    for q in range(n_row // 2):
        both = jnp.dot(xt, tiles_ref[:, 2 * q * block:2 * (q + 1) * block], preferred_element_type=F32).astype(BF16)
        mir_out[2 * q] = both[:, :block]
        mir_out[2 * q + 1] = both[:, block:]
    for t in range(n_row - 1):
        p = row_order(t)
        d = row_offset(p)
        send(mir_out.at[p], mir_in.at[d], s_mir.at[d], r_mir.at[d], (p, c))

    y = sum_out[rows_of(z), :].astype(F32)
    for d in range(1, n_z):
        copy(sum_in.at[d - 1], sum_in.at[d - 1], s_sum.at[d - 1], r_sum.at[d - 1], mate_id).wait_recv()
        y = y + sum_in[d - 1].astype(F32)
    yt = mir_out[r].astype(F32)
    for d in range(1, n_row):
        copy(mir_in.at[d - 1], mir_in.at[d - 1], s_mir.at[d - 1], r_mir.at[d - 1], mate_id).wait_recv()
        yt = yt + mir_in[d - 1].astype(F32)
    y = y + yt.T

    high = y.astype(BF16)
    low = (y - high.astype(F32)).astype(BF16)
    w = w_ref[...]
    pre = (
        jnp.dot(high, w, preferred_element_type=F32)
        + jnp.dot(low, w, preferred_element_type=F32)
        + bias_ref[...].reshape(1, -1)
    )
    act, slope = gelu_parts(pre)
    act_ref[...] = act.astype(BF16)
    grad = (cot_ref[...].astype(F32) * slope).astype(BF16)
    local = jnp.dot(high.T, grad, preferred_element_type=F32) + jnp.dot(low.T, grad, preferred_element_type=F32)
    bias_sum = jnp.sum(grad.astype(F32), axis=0, keepdims=True)

    f_out = grad.shape[1]
    h = local.shape[0] // 2
    line = lax.broadcasted_iota(jnp.int32, (16, f_out), 0)

    def packed(weight_terms, bias_terms):
        upper = bias_terms.astype(BF16).astype(F32)
        tail = jnp.where(line == 0, upper, jnp.where(line == 1, bias_terms - upper, 0.0))
        return jnp.concatenate([weight_terms, tail], axis=0).astype(BF16)

    def summed(ref):
        total = functools.reduce(lambda a, b: a + b, [ref[i].astype(F32) for i in range(ref.shape[0])])
        return total[:h, :], total[h:h + 1, :] + total[h + 1:h + 2, :]

    for j in range(2):
        pair_out[j, :h, :] = local[j * h:(j + 1) * h, :]
        pair_out[j, h:, :] = jnp.broadcast_to(bias_sum, (8, f_out))
    send(pair_out.at[mate], pair_in, s_1.at[0], r_1.at[0], mate_id)
    copy(pair_in, pair_in, s_1.at[0], r_1.at[0], mate_id).wait_recv()
    both = pair_out[core] + pair_in[...]
    over_z[z] = packed(both[:h, :], both[h:h + 1, :])
    for t in range(n_z - 1):
        p = z_order(t)
        send(over_z.at[z], over_z.at[z], s_2.at[z_offset(p)], r_2.at[z_offset(p)], (r, p * 2 + core))
    for d in range(1, n_z):
        slot = over_z.at[z_at(n_z - d)]
        copy(slot, slot, s_2.at[d - 1], r_2.at[d - 1], mate_id).wait_recv()
    over_row[r] = packed(*summed(over_z))
    for t in range(n_row - 1):
        p = row_order(t)
        send(over_row.at[r], over_row.at[r], s_3.at[row_offset(p)], r_3.at[row_offset(p)], (p, c))
    for d in range(1, n_row):
        slot = over_row.at[row_at(n_row - d)]
        copy(slot, slot, s_3.at[d - 1], r_3.at[d - 1], mate_id).wait_recv()
    weight_sum, bias_total = summed(over_row)
    bg_ref[...] = bias_total
    final[core] = weight_sum
    send(final.at[core], final.at[core], s_4.at[0], r_4.at[0], mate_id)
    slot = final.at[mate]
    copy(slot, slot, s_4.at[0], r_4.at[0], mate_id).wait_recv()
    for j in range(2):
        wg_ref[j * h:(j + 1) * h, :] = final[j]
    for one in sends:
        one.wait_send()


def finish(act_ref, wg_ref, bg_ref, act_out, wg_out, bg_out, sems):
    copies = [
        pltpu.make_async_copy(src, dst, sems.at[i])
        for i, (src, dst) in enumerate(((act_ref, act_out), (wg_ref, wg_out), (bg_ref, bg_out)))
    ]
    for one in copies:
        one.start()
    for one in copies:
        one.wait()


def on_device(n_row, n_col, x_feats, weight, bias, block_values, block_rows, block_cols, block_counts, cotangent):
    slots, block = block_values.shape[2], block_values.shape[-1]
    nodes, f_in = x_feats.shape
    f_out = weight.shape[1]
    assert nodes == block and slots <= 256 and n_row * n_col <= 256
    assert n_col % 2 == 0 and n_row % 2 == 0 and n_row & (n_row - 1) == 0
    tiles = n_row * n_col
    vmem = pl.BlockSpec(memory_space=pltpu.VMEM)
    n_z = n_col // 2
    half = f_in // 2
    pairs = []
    for count in (n_row - 1, n_z - 1, n_z, 1, n_z - 1, n_row - 1, 1, n_z - 1, n_row - 1, 1):
        pairs += [pltpu.SemaphoreType.DMA((count,))] * 2
    act, weight_grad, bias_grad = pl.pallas_call(
        functools.partial(layer, n_row, n_col),
        out_shape=(
            jax.ShapeDtypeStruct((nodes, f_out), BF16),
            jax.ShapeDtypeStruct((f_in, f_out), F32),
            jax.ShapeDtypeStruct((1, f_out), F32),
        ),
        in_specs=[pl.BlockSpec(memory_space=pltpu.HBM)] * 8,
        out_specs=(vmem, vmem, vmem),
        scratch_shapes=[
            pltpu.VMEM(block_rows.shape[1:], jnp.int32),
            pltpu.VMEM(block_cols.shape[1:], jnp.int32),
            pltpu.VMEM(block_counts.shape, jnp.int32),
            pltpu.VMEM(x_feats.shape, BF16),
            pltpu.VMEM(weight.shape, BF16),
            pltpu.VMEM(bias.shape, F32),
            pltpu.VMEM(cotangent.shape, BF16),
            pltpu.SemaphoreType.DMA((7,)),
            pltpu.VMEM((slots, block, block), BF16),
            pltpu.VMEM((slots, block, block), BF16),
            pltpu.VMEM((n_col * block, n_row * block), BF16),
            pltpu.VMEM((8, 256), jnp.int32),
            pltpu.VMEM((8, 256), jnp.int32),
            pltpu.SMEM((8, 256), jnp.int32),
            pltpu.SemaphoreType.DMA,
            pltpu.SemaphoreType.DMA,
            pltpu.VMEM((n_row * block, f_in), BF16),
            pltpu.VMEM((n_col, f_in, block), BF16),
            pltpu.VMEM((n_z * block, f_in), BF16),
            pltpu.VMEM((n_z * block, f_in), BF16),
            pltpu.VMEM((n_z * block, f_in), BF16),
            pltpu.VMEM((n_z - 1, block, f_in), BF16),
            pltpu.VMEM((n_row, f_in, block), BF16),
            pltpu.VMEM((n_row - 1, f_in, block), BF16),
            pltpu.VMEM((2, half + 8, f_out), F32),
            pltpu.VMEM((half + 8, f_out), F32),
            pltpu.VMEM((n_z, half + 16, f_out), BF16),
            pltpu.VMEM((n_row, half + 16, f_out), BF16),
            pltpu.VMEM((2, half, f_out), F32),
            *pairs,
        ],
        compiler_params=pltpu.CompilerParams(
            collective_id=0, has_side_effects=True, vmem_limit_bytes=58 * MIB
        ),
        cost_estimate=pl.CostEstimate(
            flops=4 * tiles * block * block * f_in, bytes_accessed=tiles * block * block * 2, transcendentals=0
        ),
        name="layer",
    )(block_rows, block_cols, block_counts, block_values, x_feats, weight, bias, cotangent)
    act, weight_grad, bias_grad = pl.pallas_call(
        finish,
        out_shape=tuple(jax.ShapeDtypeStruct(a.shape, a.dtype) for a in (act, weight_grad, bias_grad)),
        in_specs=[vmem] * 3,
        out_specs=(pl.BlockSpec(memory_space=pl.ANY),) * 3,
        scratch_shapes=[pltpu.SemaphoreType.DMA((3,))],
        name="finish",
    )(act, weight_grad, bias_grad)
    return act, weight_grad, bias_grad.reshape(f_out)


def solution(mesh):
    in_specs = (
        P(("col", "row"), None),
        P(),
        P(),
        P("row", "col", None, None, None),
        P("row", "col", None),
        P("row", "col", None),
        P("row", "col"),
        P(("col", "row"), None),
    )
    out_specs = (P(("col", "row"), None), P(), P())
    return jax.shard_map(
        functools.partial(on_device, mesh.shape["row"], mesh.shape["col"]),
        mesh=mesh, in_specs=in_specs, out_specs=out_specs, check_vma=False,
    )
```

```python
import functools

import jax
import jax.numpy as jnp
from jax import lax
from jax.experimental import pallas as pl
from jax.experimental.pallas import tpu as pltpu
from jax.sharding import PartitionSpec as P

F32 = jnp.float32
BF16 = jnp.bfloat16
MESH = pl.DeviceIdType.MESH
MIB = 1024 * 1024


def gelu_parts(pre):
    cdf = 0.5 * (1.0 + lax.erf(pre * 0.7071067811865476))
    dens = jnp.exp(-0.5 * pre * pre) * 0.3989422804014327
    return (pre * cdf, cdf + pre * dens)


def sort_slots(n_row, n_col, rows_ref, cols_ref, count_ref, keys, order):
    slots = rows_ref.shape[-1]
    log_row = n_row.bit_length() - 1
    row = jnp.right_shift(rows_ref[...], log_row)
    place = jnp.bitwise_and(row, 1) * (n_col // 2) + jnp.right_shift(row, 1)
    tile = place * n_row + jnp.bitwise_and(cols_ref[...], n_row - 1)
    index = lax.broadcasted_iota(jnp.int32, (1, slots), 1)
    tile = jnp.where(index < count_ref[...], tile, n_row * n_col)
    keys[...] = n_row * n_col * 256 + lax.broadcasted_iota(jnp.int32, keys.shape, 1)
    keys[0:1, 0:slots] = tile * 256 + index
    along = jnp.broadcast_to(keys[0:1, :], (256, 256))
    down = along.T
    rank = jnp.sum((along < down).astype(jnp.int32), axis=1, keepdims=True)
    lane = lax.broadcasted_iota(jnp.int32, (256, 256), 1)
    order[0:1, :] = jnp.sum(jnp.where(rank == lane, down, 0), axis=0, keepdims=True)
    order[1:2, :] = jnp.sum((jnp.right_shift(down, 8) <= lane).astype(jnp.int32), axis=0, keepdims=True)
    order[2:, :] = jnp.zeros((order.shape[0] - 2, 256), jnp.int32)


def build_tiles(n_row, n_col, order, held, runs, tiles_ref):
    slots, block = held.shape[0], held.shape[1]

    def step(i, carry):
        total, before = carry
        key = order[0, i]
        tile = jnp.right_shift(key, 8)
        slot = jnp.minimum(jnp.bitwise_and(key, 255), slots - 1)
        total = jnp.where(tile == before, total, 0.0) + held[slot].astype(F32)
        runs[i] = total.astype(BF16)
        return total, tile

    lax.fori_loop(0, slots, step, (jnp.zeros((block, block), F32), jnp.int32(-1)), unroll=4)

    def place(p, before):
        for q in range(n_row):
            end = order[1, p * n_row + q]
            value = runs[jnp.maximum(end - 1, 0)]
            rows = pl.ds(pl.multiple_of(p * block, block), block)
            tiles_ref[rows, q * block:(q + 1) * block] = jnp.where(end > before, value, jnp.zeros_like(value))
            before = end
        return before

    lax.fori_loop(0, n_col, place, jnp.int32(0))


def layer(
    n_row, n_col, rows_hbm, cols_hbm, count_hbm, values_hbm, x_hbm, w_hbm, bias_hbm, cot_hbm,
    act_ref, wg_ref, bg_ref,
    rows_ref, cols_ref, count_ref, x_ref, w_ref, bias_ref, cot_ref, input_sems,
    held, runs, tiles_ref, keys, order, order_smem, values_sem, order_sem,
    xcol, xrow, half_out, half_in, sum_out, sum_in, mir_out, mir_in, pair_out, pair_in, over_z, over_row, final,
    s_xrow, r_xrow, s_xz, r_xz, s_xp, r_xp, s_half, r_half, s_sum, r_sum, s_mir, r_mir,
    s_1, r_1, s_2, r_2, s_3, r_3, s_4, r_4,
):
    r = lax.axis_index("row")
    c = lax.axis_index("col")
    block = x_ref.shape[0]
    n_z = n_col // 2
    z = lax.div(c, 2)
    core = lax.rem(c, 2)
    mate = 1 - core
    mate_id = (r, z * 2 + mate)
    here = core * n_z + z
    sends = []

    def rows_of(index):
        return pl.ds(pl.multiple_of(index * block, block), block)

    def copy(src, dst, send, recv, device):
        return pltpu.make_async_remote_copy(
            src_ref=src, dst_ref=dst, send_sem=send, recv_sem=recv, device_id=device, device_id_type=MESH
        )

    def send(src, dst, s, t, device):
        one = copy(src, dst, s, t, device)
        one.start()
        sends.append(one)

    def row_order(t):
        self_at = lax.rem(2 * r + 1, n_row)
        t = jnp.where(t < self_at, t, t + 1)
        return lax.rem(2 * n_row - 1 - r + t, n_row)

    def z_order(t):
        up = jnp.where(n_z - 1 - t > z, n_z - 1 - t, n_z - 2 - t)
        down = jnp.where(t < z, t, t + 1)
        return jnp.where(z < n_z // 2, up, down)

    def row_offset(p):
        return lax.rem(p - r + n_row, n_row) - 1

    def z_offset(p):
        return lax.rem(p - z + n_z, n_z) - 1

    def row_at(d):
        return lax.rem(r + d, n_row)

    def z_at(d):
        return lax.rem(z + d, n_z)

    barrier = pltpu.get_barrier_semaphore()
    for d in range(1, n_row):
        pl.semaphore_signal(barrier, inc=1, device_id=(row_at(d), c), device_id_type=MESH)
    for d in range(1, n_z):
        pl.semaphore_signal(barrier, inc=1, device_id=(r, z_at(d) * 2 + core), device_id_type=MESH)
    pl.semaphore_signal(barrier, inc=1, device_id=mate_id, device_id_type=MESH)
    inputs = [
        pltpu.make_async_copy(src, dst, input_sems.at[i])
        for i, (src, dst) in enumerate((
            (x_hbm, x_ref), (rows_hbm.at[0], rows_ref), (cols_hbm.at[0], cols_ref), (count_hbm, count_ref),
            (w_hbm, w_ref), (bias_hbm, bias_ref), (cot_hbm, cot_ref),
        ))
    ]
    for one in inputs:
        one.start()
    fetch = pltpu.make_async_copy(values_hbm.at[0, 0], held, values_sem)
    fetch.start()
    for one in inputs:
        one.wait()
    x = x_ref[...]
    xcol[rows_of(r), :] = x
    xrow[here] = x.T
    sort_slots(n_row, n_col, rows_ref, cols_ref, count_ref, keys, order)
    to_smem = pltpu.make_async_copy(order, order_smem, order_sem)
    to_smem.start()
    pl.semaphore_wait(barrier, n_row + n_z - 1)

    for t in range(n_z - 1):
        p = z_order(t)
        send(xrow.at[here], xrow.at[here], s_xz.at[z_offset(p)], r_xz.at[z_offset(p)], (r, p * 2 + core))
    for t in range(n_row - 1):
        p = row_order(t)
        d = row_offset(p)
        send(xcol.at[rows_of(r)], xcol.at[rows_of(r)], s_xrow.at[d], r_xrow.at[d], (p, c))
    send(xrow.at[here], xrow.at[here], s_xp.at[0], r_xp.at[0], mate_id)

    to_smem.wait()
    fetch.wait()
    build_tiles(n_row, n_col, order_smem, held, runs, tiles_ref)

    for d in range(1, n_row):
        slot = xcol.at[rows_of(row_at(n_row - d))]
        copy(slot, slot, s_xrow.at[d - 1], r_xrow.at[d - 1], (row_at(d), c)).wait_recv()

    span = n_z * block
    there = tiles_ref[pl.ds(pl.multiple_of(mate * span, span), span), :]
    xc = xcol[...]
    half_out[...] = jnp.dot(there, xc, preferred_element_type=F32).astype(BF16)
    send(half_out, half_in, s_half.at[0], r_half.at[0], mate_id)
    mine = tiles_ref[pl.ds(pl.multiple_of(core * span, span), span), :]
    own = jnp.dot(mine, xc, preferred_element_type=F32)

    for d in range(1, n_z):
        slot = xrow.at[core * n_z + z_at(n_z - d)]
        copy(slot, slot, s_xz.at[d - 1], r_xz.at[d - 1], mate_id).wait_recv()
        send(slot, slot, s_xp.at[d], r_xp.at[d], mate_id)

    copy(half_out, half_in, s_half.at[0], r_half.at[0], mate_id).wait_recv()
    total = (own + half_in[...].astype(F32)).astype(BF16)
    sum_out[...] = total
    for t in range(n_z - 1):
        p = z_order(t)
        d = z_offset(p)
        send(sum_out.at[rows_of(p)], sum_in.at[d], s_sum.at[d], r_sum.at[d], (r, p * 2 + core))

    for d in range(n_z):
        slot = xrow.at[mate * n_z + z_at(n_z - d)]
        copy(slot, slot, s_xp.at[d], r_xp.at[d], mate_id).wait_recv()

    xt = jnp.concatenate([xrow[i] for i in range(n_col)], axis=1)
    for q in range(n_row // 2):
        both = jnp.dot(xt, tiles_ref[:, 2 * q * block:2 * (q + 1) * block], preferred_element_type=F32).astype(BF16)
        mir_out[2 * q] = both[:, :block]
        mir_out[2 * q + 1] = both[:, block:]
    for t in range(n_row - 1):
        p = row_order(t)
        d = row_offset(p)
        send(mir_out.at[p], mir_in.at[d], s_mir.at[d], r_mir.at[d], (p, c))

    y = sum_out[rows_of(z), :].astype(F32)
    for d in range(1, n_z):
        copy(sum_in.at[d - 1], sum_in.at[d - 1], s_sum.at[d - 1], r_sum.at[d - 1], mate_id).wait_recv()
        y = y + sum_in[d - 1].astype(F32)
    yt = mir_out[r].astype(F32)
    for d in range(1, n_row):
        copy(mir_in.at[d - 1], mir_in.at[d - 1], s_mir.at[d - 1], r_mir.at[d - 1], mate_id).wait_recv()
        yt = yt + mir_in[d - 1].astype(F32)
    y = y + yt.T

    high = y.astype(BF16)
    low = (y - high.astype(F32)).astype(BF16)
    w = w_ref[...]
    pre = (
        jnp.dot(high, w, preferred_element_type=F32)
        + jnp.dot(low, w, preferred_element_type=F32)
        + bias_ref[...].reshape(1, -1)
    )
    act, slope = gelu_parts(pre)
    act_ref[...] = act.astype(BF16)
    grad = (cot_ref[...].astype(F32) * slope).astype(BF16)
    local = jnp.dot(high.T, grad, preferred_element_type=F32) + jnp.dot(low.T, grad, preferred_element_type=F32)
    bias_sum = jnp.sum(grad.astype(F32), axis=0, keepdims=True)

    f_out = grad.shape[1]
    h = local.shape[0] // 2
    line = lax.broadcasted_iota(jnp.int32, (16, f_out), 0)

    def packed(weight_terms, bias_terms):
        upper = bias_terms.astype(BF16).astype(F32)
        tail = jnp.where(line == 0, upper, jnp.where(line == 1, bias_terms - upper, 0.0))
        return jnp.concatenate([weight_terms, tail], axis=0).astype(BF16)

    def summed(ref):
        total = functools.reduce(lambda a, b: a + b, [ref[i].astype(F32) for i in range(ref.shape[0])])
        return total[:h, :], total[h:h + 1, :] + total[h + 1:h + 2, :]

    for j in range(2):
        pair_out[j, :h, :] = local[j * h:(j + 1) * h, :]
        pair_out[j, h:, :] = jnp.broadcast_to(bias_sum, (8, f_out))
    send(pair_out.at[mate], pair_in, s_1.at[0], r_1.at[0], mate_id)
    copy(pair_in, pair_in, s_1.at[0], r_1.at[0], mate_id).wait_recv()
    both = pair_out[core] + pair_in[...]
    over_z[z] = packed(both[:h, :], both[h:h + 1, :])
    for t in range(n_z - 1):
        p = z_order(t)
        send(over_z.at[z], over_z.at[z], s_2.at[z_offset(p)], r_2.at[z_offset(p)], (r, p * 2 + core))
    for d in range(1, n_z):
        slot = over_z.at[z_at(n_z - d)]
        copy(slot, slot, s_2.at[d - 1], r_2.at[d - 1], mate_id).wait_recv()
    over_row[r] = packed(*summed(over_z))
    for t in range(n_row - 1):
        p = row_order(t)
        send(over_row.at[r], over_row.at[r], s_3.at[row_offset(p)], r_3.at[row_offset(p)], (p, c))
    for d in range(1, n_row):
        slot = over_row.at[row_at(n_row - d)]
        copy(slot, slot, s_3.at[d - 1], r_3.at[d - 1], mate_id).wait_recv()
    weight_sum, bias_total = summed(over_row)
    bg_ref[...] = bias_total
    final[core] = weight_sum
    send(final.at[core], final.at[core], s_4.at[0], r_4.at[0], mate_id)
    slot = final.at[mate]
    copy(slot, slot, s_4.at[0], r_4.at[0], mate_id).wait_recv()
    for j in range(2):
        wg_ref[j * h:(j + 1) * h, :] = final[j]
    for one in sends:
        one.wait_send()


def finish(act_ref, wg_ref, bg_ref, act_out, wg_out, bg_out):
    act_out[...] = act_ref[...]
    wg_out[...] = wg_ref[...]
    bg_out[...] = bg_ref[...]


def on_device(n_row, n_col, x_feats, weight, bias, block_values, block_rows, block_cols, block_counts, cotangent):
    slots, block = block_values.shape[2], block_values.shape[-1]
    nodes, f_in = x_feats.shape
    f_out = weight.shape[1]
    assert nodes == block and slots <= 256 and n_row * n_col <= 256
    assert n_col % 2 == 0 and n_row % 2 == 0 and n_row & (n_row - 1) == 0
    tiles = n_row * n_col
    vmem = pl.BlockSpec(memory_space=pltpu.VMEM)
    n_z = n_col // 2
    half = f_in // 2
    pairs = []
    for count in (n_row - 1, n_z - 1, n_z, 1, n_z - 1, n_row - 1, 1, n_z - 1, n_row - 1, 1):
        pairs += [pltpu.SemaphoreType.DMA((count,))] * 2
    act, weight_grad, bias_grad = pl.pallas_call(
        functools.partial(layer, n_row, n_col),
        out_shape=(
            jax.ShapeDtypeStruct((nodes, f_out), BF16),
            jax.ShapeDtypeStruct((f_in, f_out), F32),
            jax.ShapeDtypeStruct((1, f_out), F32),
        ),
        in_specs=[pl.BlockSpec(memory_space=pltpu.HBM)] * 8,
        out_specs=(vmem, vmem, vmem),
        scratch_shapes=[
            pltpu.VMEM(block_rows.shape[1:], jnp.int32),
            pltpu.VMEM(block_cols.shape[1:], jnp.int32),
            pltpu.VMEM(block_counts.shape, jnp.int32),
            pltpu.VMEM(x_feats.shape, BF16),
            pltpu.VMEM(weight.shape, BF16),
            pltpu.VMEM(bias.shape, F32),
            pltpu.VMEM(cotangent.shape, BF16),
            pltpu.SemaphoreType.DMA((7,)),
            pltpu.VMEM((slots, block, block), BF16),
            pltpu.VMEM((slots, block, block), BF16),
            pltpu.VMEM((n_col * block, n_row * block), BF16),
            pltpu.VMEM((8, 256), jnp.int32),
            pltpu.VMEM((8, 256), jnp.int32),
            pltpu.SMEM((8, 256), jnp.int32),
            pltpu.SemaphoreType.DMA,
            pltpu.SemaphoreType.DMA,
            pltpu.VMEM((n_row * block, f_in), BF16),
            pltpu.VMEM((n_col, f_in, block), BF16),
            pltpu.VMEM((n_z * block, f_in), BF16),
            pltpu.VMEM((n_z * block, f_in), BF16),
            pltpu.VMEM((n_z * block, f_in), BF16),
            pltpu.VMEM((n_z - 1, block, f_in), BF16),
            pltpu.VMEM((n_row, f_in, block), BF16),
            pltpu.VMEM((n_row - 1, f_in, block), BF16),
            pltpu.VMEM((2, half + 8, f_out), F32),
            pltpu.VMEM((half + 8, f_out), F32),
            pltpu.VMEM((n_z, half + 16, f_out), BF16),
            pltpu.VMEM((n_row, half + 16, f_out), BF16),
            pltpu.VMEM((2, half, f_out), F32),
            *pairs,
        ],
        compiler_params=pltpu.CompilerParams(
            collective_id=0, has_side_effects=True, vmem_limit_bytes=58 * MIB
        ),
        cost_estimate=pl.CostEstimate(
            flops=4 * tiles * block * block * f_in, bytes_accessed=tiles * block * block * 2, transcendentals=0
        ),
        name="layer",
    )(block_rows, block_cols, block_counts, block_values, x_feats, weight, bias, cotangent)
    act, weight_grad, bias_grad = pl.pallas_call(
        finish,
        out_shape=tuple(jax.ShapeDtypeStruct(a.shape, a.dtype) for a in (act, weight_grad, bias_grad)),
        in_specs=[vmem] * 3,
        out_specs=(vmem,) * 3,
        name="finish",
    )(act, weight_grad, bias_grad)
    return act, weight_grad, bias_grad.reshape(f_out)


def solution(mesh):
    in_specs = (
        P(("col", "row"), None),
        P(),
        P(),
        P("row", "col", None, None, None),
        P("row", "col", None),
        P("row", "col", None),
        P("row", "col"),
        P(("col", "row"), None),
    )
    out_specs = (P(("col", "row"), None), P(), P())
    return jax.shard_map(
        functools.partial(on_device, mesh.shape["row"], mesh.shape["col"]),
        mesh=mesh, in_specs=in_specs, out_specs=out_specs, check_vma=False,
    )
```
